128 devices in a mesh: kpt: 16 (over z, y_hi, core), row: 8 (over x, y_lo).
Axes of the slice: x: 4, y: 4 (y_hi: 2, y_lo: 2; y = y_hi * 2 + y_lo), z: 4, core: 2. Of those that a mesh axis runs over, the one named last changes fastest.
Arguments:
- occ_orbitals: bfloat16 [64, 2048, 128], P('kpt', 'row'), may hold values from -0.5 to 0.5
- virt_orbitals: bfloat16 [64, 2048, 256], P('kpt', 'row'), may hold values from -0.375 to 0.375
- occ_gap: bfloat16 [64, 128], P('kpt'), may hold values from 0.049804688 to 3
- virt_gap: bfloat16 [64, 256], P('kpt'), may hold values from 0.049804688 to 3
- partner: int32 [3, 64], replicated, may hold values from 0 to 63, as said below
Outputs:
- chi: float32 [3, 4, 2048, 2048], P(None, None, 'row', 'kpt')
The draws below stay inside these ranges and needn't reach their ends.
Inputs may be any that keep to these rules, and one draw needn't show every extreme that they name: For each transfer q there is a shift s_q of 0 to 4 with partner[q, k] = (k - s_q) mod 64 for every k; the shifts of different transfers differ, and some transfer has s_q = 4.
All inputs are finite; a program needn't handle non-finite values.
Results may differ from the reference program's by a relative error of at most 0.0003.
Values may be sent and summed in bfloat16 or wider, within the bound.
No kernel may reach another device: no remote copies, remote signals or barrier semaphores. Data moves between devices by JAX's collectives and lax.ppermute only.
A program may use at most 320 MiB of HBM per device.

```python
import math
import jax
import jax.numpy as jnp
from jax import lax

NP = 2048
NOCC = 128
NV = 256
NTAU = 4
QWIN = 3
K_DEV = 4
K = 64


def draw_partner(key, part):
    others = jax.random.permutation(jax.random.fold_in(key, 7), jnp.arange(K_DEV, dtype=jnp.int32))[:QWIN - 1].astype(jnp.int32)
    shift_values = jnp.concatenate([jnp.full((1,), K_DEV, jnp.int32), others])
    shift_values = jax.random.permutation(jax.random.fold_in(key, 11), shift_values).astype(jnp.int32)
    momentum_ids = jnp.arange(K, dtype=jnp.int32)
    return ((momentum_ids[None, :] - shift_values[:, None]) % K).astype(jnp.int32)


def levels(rng, extent, pieces, least, high):
    def one(dim, blocks):
        steps = jax.random.uniform(jax.random.fold_in(jax.random.fold_in(rng, 6), dim), (blocks,), jnp.float32, least / len(pieces), high / len(pieces))
        return jnp.repeat(jnp.exp(steps), extent[dim] // blocks).reshape((-1,) + (1,) * (len(extent) - dim - 1))

    gain = one(*pieces[0])
    for cut in pieces[1:]:
        gain = gain * one(*cut)
    return gain


def normal_values(own_key, extent, deviation, most, pieces=(), kind=jnp.bfloat16):
    drawn = jax.random.normal(own_key, extent, jnp.float32) * deviation
    if len(pieces) > 0:
        drawn = levels(own_key, extent, pieces, -0.22, 0.18) * drawn
    return jnp.clip(drawn, min=-most, max=most).astype(kind)


def setup_inputs(seed: int = 0) -> dict:
    seeds = jax.random.split(jax.random.key(seed), 6)
    occ_orbitals = normal_values(seeds[0], (K, NP, NOCC), NOCC ** -0.5, 0.5, ((0, 16), (1, 8)))
    virt_orbitals = normal_values(seeds[1], (K, NP, NV), NV ** -0.5, 0.375, ((0, 16), (1, 8)))
    occ_gap = jnp.clip(jnp.exp(math.log(3.0) - 4.0982585 * jax.random.uniform(seeds[2], (K, NOCC), jnp.float32) ** levels(seeds[2], (K, NOCC), ((0, 16),), -0.2, 0.2)), 0.049804688, 3.0).astype(jnp.bfloat16)
    virt_gap = jnp.clip(jnp.exp(math.log(3.0) - 4.0982585 * jax.random.uniform(seeds[3], (K, NV), jnp.float32) ** levels(seeds[3], (K, NV), ((0, 16),), -0.2, 0.2)), 0.049804688, 3.0).astype(jnp.bfloat16)
    partner = draw_partner(jax.random.fold_in(seeds[5], 71), 0)
    return dict(occ_orbitals=occ_orbitals, virt_orbitals=virt_orbitals, occ_gap=occ_gap, virt_gap=virt_gap, partner=partner)


def reference(occ_orbitals, virt_orbitals, occ_gap, virt_gap, partner):
    tau_values = 0.25 * 2.0 ** jnp.arange(NTAU, dtype=jnp.float32)
    momentum_ids = jnp.arange(K, dtype=jnp.int32)
    results = []
    for step_index in range(NTAU):
        moment = tau_values[step_index]

        def accumulate(running, momentum):
            occ_rows = occ_orbitals[momentum]
            occ_factor = jnp.exp(-occ_gap[momentum].astype(jnp.float32) * moment)
            occ_panel = (occ_rows.astype(jnp.float32) * occ_factor[None, :]).astype(jnp.bfloat16)
            occ_green = jnp.dot(occ_panel, occ_rows.T, preferred_element_type=jnp.float32)
            updated = []
            for transfer in range(QWIN):
                partner_id = partner[transfer, momentum]
                virt_rows = virt_orbitals[partner_id]
                virt_factor = jnp.exp(-virt_gap[partner_id].astype(jnp.float32) * moment)
                virt_panel = (virt_rows.astype(jnp.float32) * virt_factor[None, :]).astype(jnp.bfloat16)
                virt_green = jnp.dot(virt_panel, virt_rows.T, preferred_element_type=jnp.float32)
                updated.append(running[transfer] + occ_green * virt_green)
            return jnp.stack(updated), None

        running, _ = lax.scan(accumulate, jnp.zeros((QWIN, NP, NP), jnp.float32), momentum_ids)
        results.append(running)
    return jnp.stack(results, axis=1)
```

```python
import jax
import jax.numpy as jnp
from jax import lax
from jax.experimental import pallas as pl
from jax.experimental.pallas import tpu as pltpu
from jax.sharding import Mesh, PartitionSpec as P

AXES = ("z", "yh", "c", "x", "yl")
NTAU = 4
NT_DIMS = (((1,), (1,)), ((), ()))


def routes(target):
    def linear(z, yh, c, x, yl):
        return (((z % 4) * 2 + yh) * 2 + c) * 8 + (x % 4) * 2 + yl

    return [
        (linear(z, yh, c, x, yl), linear(*target(z, yh, c, x, yl)))
        for z in range(4)
        for yh in range(2)
        for c in range(2)
        for x in range(4)
        for yl in range(2)
    ]


def send(block, target):
    return lax.ppermute(block, AXES, routes(target))


def kernel(shift, fac, row_blk, col_blk, out, vbuf, obuf, acc):
    step = pl.program_id(0)
    par = (step + 1) % 2

    @pl.when(step == 0)
    def _():
        acc[...] = jnp.zeros_like(acc)

    for i in range(4):
        col = col_blk[0, i].astype(jnp.float32)
        virt = jnp.concatenate(
            [(col[:, 128:] * fac[0, i, t : t + 1, 128:]).astype(jnp.bfloat16) for t in range(NTAU)], 0
        )
        vbuf[par * 4 + i] = lax.dot_general(
            virt, row_blk[0, i, :, 128:], NT_DIMS, preferred_element_type=jnp.float32
        )
        occ = jnp.concatenate(
            [(col[:, :128] * fac[0, i, t : t + 1, :128]).astype(jnp.bfloat16) for t in range(NTAU)], 0
        )
        obuf[i] = lax.dot_general(
            occ, row_blk[0, i, :, :128], NT_DIMS, preferred_element_type=jnp.float32
        )

    @pl.when(step > 0)
    def _():
        height = 16

        @pl.loop(0, 512 // height)
        def _(g):
            rows = pl.ds(pl.multiple_of(g * height, height), height)
            occs = [obuf[i, rows, :] for i in range(4)]
            for q in range(3):
                total = acc[q, rows, :]
                for i in range(4):
                    total = total + occs[i] * vbuf[(par * 4 + i - shift[q] + 8) % 8, rows, :]
                acc[q, rows, :] = total

    @pl.when(step == 16)
    def _():
        for q in range(3):
            for t in range(NTAU):
                out[q, t] = acc[q, t * 128 : (t + 1) * 128, :].T


def slab_of(step):
    return (step + 15) % 16


def held_at(step):
    j = slab_of(step)
    return (j // 4) * 4 + (j % 2) * 2 + (j // 2) % 2


def polarizability(shift, fac, row_pts, col_pts):
    spec = pltpu.PrefetchScalarGridSpec(
        num_scalar_prefetch=1,
        grid=(17,),
        in_specs=[
            pl.BlockSpec((1, 4, NTAU, 384), lambda s, _: (slab_of(s), 0, 0, 0)),
            pl.BlockSpec((1, 4, 256, 384), lambda s, _: (held_at(s), 0, 0, 0)),
            pl.BlockSpec((1, 4, 128, 384), lambda s, _: (held_at(s), 0, 0, 0)),
        ],
        out_specs=pl.BlockSpec((3, NTAU, 256, 128), lambda s, _: (0, 0, 0, 0)),
        scratch_shapes=[
            pltpu.VMEM((8, 512, 256), jnp.float32),
            pltpu.VMEM((4, 512, 256), jnp.float32),
            pltpu.VMEM((3, 512, 256), jnp.float32),
        ],
    )
    return pl.pallas_call(
        kernel,
        grid_spec=spec,
        out_shape=jax.ShapeDtypeStruct((3, NTAU, 256, 128), jnp.float32),
        compiler_params=pltpu.CompilerParams(vmem_limit_bytes=40 * 2**20),
    )(shift, fac, row_pts, col_pts)


def on_device(occ_orbitals, virt_orbitals, occ_gap, virt_gap, partner):
    z, yh, c, x, yl = (lax.axis_index(a) for a in AXES)
    shift = (-partner[:, 0]) % 64
    own = jnp.concatenate([occ_orbitals, virt_orbitals], axis=2)
    gaps = jnp.concatenate([occ_gap, virt_gap], axis=1)
    gaps = lax.all_gather(gaps, ("z", "yh", "c"), axis=0).astype(jnp.float32)
    tau = 0.25 * 2.0 ** jnp.arange(NTAU, dtype=jnp.float32)
    fac = jnp.exp(-gaps[:, :, None, :] * tau[:, None])

    other = send(own, lambda z, yh, c, x, yl: (z, 1 - yh, c, x, yl))
    same_t = send(own, lambda z, yh, c, x, yl: (x, yl, c, z, yh))
    cross_t = send(own, lambda z, yh, c, x, yl: (x, yl, c, z, 1 - yh))

    rows_piece = jnp.where(yh == 0, jnp.stack([own, other]), jnp.stack([other, own]))
    cols_piece = jnp.where(yl == 0, jnp.stack([same_t, cross_t]), jnp.stack([cross_t, same_t]))
    row_pts = jnp.zeros((4, 2, 2, 4, 256, 384), jnp.bfloat16)
    col_pts = jnp.zeros((4, 2, 2, 4, 128, 384), jnp.bfloat16)
    way = 2 * c - 1

    def swap(block):
        return send(block, lambda z, yh, c, x, yl: (z, yh, 1 - c, x, yl))

    for step in range(4):
        mine, theirs = way * step, -way * step
        got = swap(rows_piece)
        row_pts = lax.dynamic_update_slice(row_pts, rows_piece[None, None], ((z + mine) % 4, c, 0, 0, 0, 0))
        row_pts = lax.dynamic_update_slice(row_pts, got[None, None], ((z + theirs) % 4, 1 - c, 0, 0, 0, 0))
        keep = lax.dynamic_slice_in_dim(cols_piece, c * 128, 128, 2)
        give = lax.dynamic_slice_in_dim(cols_piece, (1 - c) * 128, 128, 2)
        got = swap(give)
        col_pts = lax.dynamic_update_slice(col_pts, keep[None, None], ((x + mine) % 4, c, 0, 0, 0, 0))
        col_pts = lax.dynamic_update_slice(col_pts, got[None, None], ((x + theirs) % 4, 1 - c, 0, 0, 0, 0))
        if step < 3:
            rows_piece = send(rows_piece, lambda z, yh, c, x, yl: (z + 1 - 2 * c, yh, c, x, yl))
            cols_piece = send(cols_piece, lambda z, yh, c, x, yl: (z, yh, c, x + 1 - 2 * c, yl))
    return polarizability(
        shift, fac, row_pts.reshape(16, 4, 256, 384), col_pts.reshape(16, 4, 128, 384)
    )


def solution(mesh):
    fine = Mesh(mesh.devices.reshape(4, 2, 2, 4, 2), AXES)
    kpt, row = ("z", "yh", "c"), ("x", "yl")
    in_specs = (P(kpt, row, None), P(kpt, row, None), P(kpt, None), P(kpt, None), P())
    return jax.shard_map(
        on_device, mesh=fine, in_specs=in_specs, out_specs=P(None, None, row, kpt), check_vma=False
    )
```

```python
import jax
import jax.numpy as jnp
from jax import lax
from jax.experimental import pallas as pl
from jax.experimental.pallas import tpu as pltpu
from jax.sharding import Mesh, PartitionSpec as P

AXES = ("z", "yh", "c", "x", "yl")
NTAU = 4
TAUS = [0.25 * 2.0**t for t in range(NTAU)]
NT_DIMS = (((1,), (1,)), ((), ()))


def routes(target):
    def linear(z, yh, c, x, yl):
        return (((z % 4) * 2 + yh) * 2 + c) * 8 + (x % 4) * 2 + yl

    return [
        (linear(z, yh, c, x, yl), linear(*target(z, yh, c, x, yl)))
        for z in range(4)
        for yh in range(2)
        for c in range(2)
        for x in range(4)
        for yl in range(2)
    ]


def send(block, target):
    return lax.ppermute(block, AXES, routes(target))


def kernel(shift, slots, row_src, *refs):
    sources, (out, row_pts, col_pts, vbuf, obuf, acc, row_sems, col_sems) = refs[:16], refs[16:]
    core = slots[16]
    first = pl.multiple_of(core * 128, 128)
    points = pl.ds(pl.multiple_of(core * 16, 16), 128)
    levels = pl.ds((1 - core) * 128, 1)

    def row_copy(slab):
        return pltpu.make_async_copy(row_src.at[slab], row_pts.at[slab], row_sems.at[slab])

    def col_copy(n, slab):
        return pltpu.make_async_copy(
            sources[n].at[:, pl.ds(first, 144), :], col_pts.at[slab], col_sems.at[slab]
        )

    row_copy(15).start()
    for n in range(16):
        col_copy(n, slots[n]).start()
    for n in range(15):
        row_copy(n).start()
    acc[...] = jnp.zeros_like(acc)

    @pl.loop(0, 17)
    def _(step):
        par = (step + 1) % 2
        slab = (step + 15) % 16

        @pl.when(step < 16)
        def _():
            row_copy(slab).wait()
            col_copy(0, slab).wait()

        for i in range(4):
            col = col_pts[slab, i, points, :].astype(jnp.float32)
            gap = col_pts[slab, i, levels, :].astype(jnp.float32)
            panel = jnp.concatenate(
                [(col * jnp.exp(-gap * TAUS[t])).astype(jnp.bfloat16) for t in range(NTAU)], 0
            )
            vbuf[par * 4 + i] = lax.dot_general(
                panel[:, 128:], row_pts[slab, i, :, 128:], NT_DIMS, preferred_element_type=jnp.float32
            )
            obuf[i] = lax.dot_general(
                panel[:, :128], row_pts[slab, i, :, :128], NT_DIMS, preferred_element_type=jnp.float32
            )

        @pl.when(step > 0)
        def _():
            height = 64

            @pl.loop(0, 512 // height)
            def _(g):
                rows = pl.ds(pl.multiple_of(g * height, height), height)
                occs = [obuf[i, rows, :] for i in range(4)]
                for q in range(3):
                    total = acc[q, rows, :]
                    for i in range(4):
                        total = total + occs[i] * vbuf[(par * 4 + i - shift[q] + 8) % 8, rows, :]
                    acc[q, rows, :] = total

    for q in range(3):
        for t in range(NTAU):
            out[q, t] = acc[q, t * 128 : (t + 1) * 128, :].T


def polarizability(shift, slots, row_pts, sources):
    anywhere = pl.BlockSpec(memory_space=pl.ANY)
    scalars = pl.BlockSpec(memory_space=pltpu.SMEM)
    return pl.pallas_call(
        kernel,
        in_specs=[scalars, scalars] + [anywhere] * 17,
        out_specs=pl.BlockSpec(memory_space=pltpu.VMEM),
        scratch_shapes=[
            pltpu.VMEM((16, 4, 256, 384), jnp.bfloat16),
            pltpu.VMEM((16, 4, 144, 384), jnp.bfloat16),
            pltpu.VMEM((8, 512, 256), jnp.float32),
            pltpu.VMEM((4, 512, 256), jnp.float32),
            pltpu.VMEM((3, 512, 256), jnp.float32),
            pltpu.SemaphoreType.DMA((16,)),
            pltpu.SemaphoreType.DMA((16,)),
        ],
        out_shape=jax.ShapeDtypeStruct((3, NTAU, 256, 128), jnp.float32),
        compiler_params=pltpu.CompilerParams(vmem_limit_bytes=44 * 2**20),
    )(shift, slots, row_pts, *sources)


def on_device(occ_orbitals, virt_orbitals, occ_gap, virt_gap, partner):
    z, yh, c, x, yl = (lax.axis_index(a) for a in AXES)
    shift = (-partner[:, 0]) % 64
    own = jnp.concatenate([occ_orbitals, virt_orbitals], axis=2)
    gaps = jnp.concatenate([occ_gap, virt_gap], axis=1)
    gaps = jnp.broadcast_to(gaps[:, None, :], (4, 16, 384))
    carried = jnp.concatenate([own[:, :128], gaps, own[:, 128:]], axis=1)
    row_pts = lax.all_gather(own, ("z", "yh", "c"), axis=0)

    same = [send(carried, lambda z, yh, c, x, yl: (x, yl, c, x + z, yh))]
    cross = [send(same[0], lambda z, yh, c, x, yl: (z, yh, c, x, 1 - yl))]
    for ring in (same, cross):
        for _ in range(3):
            ring.append(send(ring[-1], lambda z, yh, c, x, yl: (z, yh, c, x + 1 - 2 * c, yl)))
    sources, slots = [], []
    for s in range(4):
        for ring, yl_held in ((same, yl), (cross, 1 - yl)):
            got = send(ring[s], lambda z, yh, c, x, yl: (z, yh, 1 - c, x, yl))
            for block, core in ((ring[s], c), (got, 1 - c)):
                sources.append(block)
                slots.append((x - z + (2 * core - 1) * s) % 4 * 4 + yl_held * 2 + core)
    slots = jnp.stack(slots + [c]).astype(jnp.int32)
    return polarizability(shift, slots, row_pts, sources)


def solution(mesh):
    fine = Mesh(mesh.devices.reshape(4, 2, 2, 4, 2), AXES)
    kpt, row = ("z", "yh", "c"), ("x", "yl")
    in_specs = (P(kpt, row, None), P(kpt, row, None), P(kpt, None), P(kpt, None), P())
    return jax.shard_map(
        on_device, mesh=fine, in_specs=in_specs, out_specs=P(None, None, row, kpt), check_vma=False
    )
```

```python
import jax
import jax.numpy as jnp
from jax import lax
from jax.experimental import pallas as pl
from jax.experimental.pallas import tpu as pltpu
from jax.sharding import Mesh, PartitionSpec as P

AXES = ("z", "yh", "c", "x", "yl")
NTAU = 4
TAUS = [0.25 * 2.0**t for t in range(NTAU)]
NT_DIMS = (((1,), (1,)), ((), ()))


def routes(target):
    def linear(z, yh, c, x, yl):
        return (((z % 4) * 2 + yh) * 2 + c) * 8 + (x % 4) * 2 + yl

    return [
        (linear(z, yh, c, x, yl), linear(*target(z, yh, c, x, yl)))
        for z in range(4)
        for yh in range(2)
        for c in range(2)
        for x in range(4)
        for yl in range(2)
    ]


def send(block, target):
    return lax.ppermute(block, AXES, routes(target))


def kernel(shift, source, *refs):
    row_src, col_src, refs = refs[:16], refs[16:32], refs[32:]
    out, row_pts, col_pts, vbuf, obuf, acc, row_sems, col_sems = refs
    core = source[32]
    first = pl.multiple_of(core * 128, 128)
    points = pl.ds(pl.multiple_of(core * 16, 16), 128)
    levels = pl.ds((1 - core) * 128, 1)

    def row_copy(n, slot):
        return pltpu.make_async_copy(row_src[n], row_pts.at[slot], row_sems.at[slot])

    def col_copy(n, slot):
        return pltpu.make_async_copy(
            col_src[n].at[:, pl.ds(first, 144), :], col_pts.at[slot], col_sems.at[slot]
        )

    def fetch(step):
        slab, slot = lax.rem(step + 15, 16), lax.rem(step, 3)
        row_from, col_from = source[slab], source[16 + slab]
        for n in range(16):

            @pl.when(row_from == n)
            def _():
                row_copy(n, slot).start()

            @pl.when(col_from == n)
            def _():
                col_copy(n, slot).start()

    fetch(0)
    fetch(1)
    acc[...] = jnp.zeros_like(acc)

    @pl.loop(0, 17)
    def _(step):
        par = lax.rem(step + 1, 2) * 4
        slot = lax.rem(step, 3)

        @pl.when(step < 15)
        def _():
            fetch(step + 2)

        row_copy(0, slot).wait()
        col_copy(0, slot).wait()
        for i in range(4):
            col = col_pts[slot, i, points, :].astype(jnp.float32)
            gap = col_pts[slot, i, levels, :].astype(jnp.float32)
            panel = jnp.concatenate(
                [(col * jnp.exp(-gap * TAUS[t])).astype(jnp.bfloat16) for t in range(NTAU)], 0
            )
            vbuf[par + i] = lax.dot_general(
                panel[:, 128:], row_pts[slot, i, :, 128:], NT_DIMS, preferred_element_type=jnp.float32
            )
            obuf[i] = lax.dot_general(
                panel[:, :128], row_pts[slot, i, :, :128], NT_DIMS, preferred_element_type=jnp.float32
            )

        @pl.when(step > 0)
        def _():
            height = 32
            for g in range(512 // height):
                rows = pl.ds(g * height, height)
                occs = [obuf[i, rows, :] for i in range(4)]
                for q in range(3):
                    total = acc[q, rows, :]
                    for i in range(4):
                        total = total + occs[i] * vbuf[lax.rem(par + i - shift[q] + 8, 8), rows, :]
                    acc[q, rows, :] = total

    for q in range(3):
        for t in range(NTAU):
            out[q, t] = acc[q, t * 128 : (t + 1) * 128, :].T


def polarizability(shift, source, pieces):
    anywhere = pl.BlockSpec(memory_space=pl.ANY)
    scalars = pl.BlockSpec(memory_space=pltpu.SMEM)
    return pl.pallas_call(
        kernel,
        in_specs=[scalars, scalars] + [anywhere] * 32,
        out_specs=pl.BlockSpec(memory_space=pltpu.VMEM),
        scratch_shapes=[
            pltpu.VMEM((3, 4, 256, 384), jnp.bfloat16),
            pltpu.VMEM((3, 4, 144, 384), jnp.bfloat16),
            pltpu.VMEM((8, 512, 256), jnp.float32),
            pltpu.VMEM((4, 512, 256), jnp.float32),
            pltpu.VMEM((3, 512, 256), jnp.float32),
            pltpu.SemaphoreType.DMA((3,)),
            pltpu.SemaphoreType.DMA((3,)),
        ],
        out_shape=jax.ShapeDtypeStruct((3, NTAU, 256, 128), jnp.float32),
        compiler_params=pltpu.CompilerParams(vmem_limit_bytes=20 * 2**20),
    )(shift, source, *[pltpu.with_memory_space_constraint(p, pltpu.HBM) for p in pieces])


def after(block, *others):
    return lax.optimization_barrier((block,) + others)[0]


def swap(block):
    return send(block, lambda z, yh, c, x, yl: (z, yh, 1 - c, x, yl))


def z_step(block, sign):
    return send(block, lambda z, yh, c, x, yl: (z + sign * (1 - 2 * c), yh, c, x, yl))


def x_step(block, sign):
    return send(block, lambda z, yh, c, x, yl: (z, yh, c, x + sign * (1 - 2 * c), yl))


def across_yh(block):
    return send(block, lambda z, yh, c, x, yl: (z, 1 - yh, c, x, yl))


def on_device(occ_orbitals, virt_orbitals, occ_gap, virt_gap, partner):
    z, yh, c, x, yl = (lax.axis_index(a) for a in AXES)
    shift = (-partner[:, 0]) % 64
    own = jnp.concatenate([occ_orbitals, virt_orbitals], axis=2)
    gaps = jnp.concatenate([occ_gap, virt_gap], axis=1)
    gaps = jnp.broadcast_to(gaps[:, None, :], (4, 16, 384))
    carried = jnp.concatenate([own[:, :128], gaps, own[:, 128:]], axis=1)

    cols = send(carried, lambda z, yh, c, x, yl: (x, yl, c, x + z, yh))
    cols_same, rows_same = [cols], [own]
    cols_cross = [send(cols, lambda z, yh, c, x, yl: (z, yh, c, x, 1 - yl))]
    for _ in range(3):
        rows_same.append(z_step(rows_same[-1], 1))
        cols_same.append(x_step(cols_same[-1], 1))
    rows_cross = [across_yh(own)]
    cols_cross.append(x_step(cols_cross[0], 1))
    rows_cross.append(z_step(rows_cross[0], 1))
    cols_cross += [x_step(cols_cross[1], 1)]
    cols_cross += [x_step(cols_cross[2], 1)]
    rows_cross += [z_step(rows_cross[1], 1)]
    rows_cross += [z_step(rows_cross[2], 1)]

    def placed(pieces, at, low):
        found = []
        for piece, offset in zip(pieces, range(4)):
            for block, core in ((piece, c), (swap(piece), 1 - c)):
                found.append((block, (at + (2 * core - 1) * offset) % 4 * 4 + low * 2 + core))
        return found

    pieces = placed(rows_same, z, yh) + placed(rows_cross, z, 1 - yh)
    pieces += placed(cols_same, x - z, yl) + placed(cols_cross, x - z, 1 - yl)
    slots = jnp.stack([slot for _, slot in pieces])
    held = jnp.arange(16)
    source = [jnp.sum((part[:, None] == held) * held[:, None], axis=0) for part in (slots[:16], slots[16:])]
    source = jnp.concatenate(source + [c[None]]).astype(jnp.int32)
    return polarizability(shift, source, [block for block, _ in pieces])


def solution(mesh):
    fine = Mesh(mesh.devices.reshape(4, 2, 2, 4, 2), AXES)
    kpt, row = ("z", "yh", "c"), ("x", "yl")
    in_specs = (P(kpt, row, None), P(kpt, row, None), P(kpt, None), P(kpt, None), P())
    return jax.shard_map(
        on_device, mesh=fine, in_specs=in_specs, out_specs=P(None, None, row, kpt), check_vma=False
    )
```

```python
import jax
import jax.numpy as jnp
from jax import lax
from jax.experimental import pallas as pl
from jax.experimental.pallas import tpu as pltpu
from jax.sharding import Mesh, PartitionSpec as P

AXES = ("z", "yh", "c", "x", "yl")
NTAU = 4
TAUS = [0.25 * 2.0**t for t in range(NTAU)]
NT_DIMS = (((1,), (1,)), ((), ()))


def routes(target):
    def linear(z, yh, c, x, yl):
        return (((z % 4) * 2 + yh) * 2 + c) * 8 + (x % 4) * 2 + yl

    return [
        (linear(z, yh, c, x, yl), linear(*target(z, yh, c, x, yl)))
        for z in range(4)
        for yh in range(2)
        for c in range(2)
        for x in range(4)
        for yl in range(2)
    ]


def send(block, target):
    return lax.ppermute(block, AXES, routes(target))


def kernel(shift, source, *refs):
    row_src, col_src, refs = refs[:16], refs[16:24], refs[24:]
    out, row_pts, col_pts, vbuf, obuf, acc, row_sems, col_sems = refs

    def row_copy(n, slot):
        return pltpu.make_async_copy(row_src[n], row_pts.at[slot], row_sems.at[slot])

    def col_copy(n, slot):
        return pltpu.make_async_copy(col_src[n // 2].at[n % 2], col_pts.at[slot, pl.ds(0, 528)], col_sems.at[slot])

    def fetch(step):
        slab, slot = lax.rem(step + 15, 16), lax.rem(step, 3)
        row_from, col_from = source[slab], source[16 + slab]
        for n in range(16):

            @pl.when(row_from == n)
            def _():
                row_copy(n, slot).start()

            @pl.when(col_from == n)
            def _():
                col_copy(n, slot).start()

    fetch(0)
    fetch(1)
    acc[...] = jnp.zeros_like(acc)

    @pl.loop(0, 17)
    def _(step):
        par = lax.rem(step + 1, 2) * 4
        slot = lax.rem(step, 3)

        @pl.when(step < 15)
        def _():
            fetch(step + 2)

        row_copy(0, slot).wait()
        col_copy(0, slot).wait()
        gaps = col_pts[slot, 512:528, :].astype(jnp.float32)
        factors = [jnp.exp(-gaps * TAUS[t]) for t in range(NTAU)]
        for i in range(4):
            col = col_pts[slot, i * 128 : (i + 1) * 128, :].astype(jnp.float32)
            panel = jnp.concatenate(
                [(col * factors[t][i : i + 1]).astype(jnp.bfloat16) for t in range(NTAU)], 0
            )
            vbuf[par + i] = lax.dot_general(
                panel[:, 128:], row_pts[slot, i, :, 128:], NT_DIMS, preferred_element_type=jnp.float32
            )
            obuf[i] = lax.dot_general(
                panel[:, :128], row_pts[slot, i, :, :128], NT_DIMS, preferred_element_type=jnp.float32
            )

        @pl.when(step > 0)
        def _():
            height = 32
            for g in range(512 // height):
                rows = pl.ds(g * height, height)
                occs = [obuf[i, rows, :] for i in range(4)]
                for q in range(3):
                    total = acc[q, rows, :]
                    for i in range(4):
                        total = total + occs[i] * vbuf[lax.rem(par + i - shift[q] + 8, 8), rows, :]
                    acc[q, rows, :] = total

    for q in range(3):
        for t in range(NTAU):
            out[q, t] = acc[q, t * 128 : (t + 1) * 128, :].T


def polarizability(shift, source, pieces):
    anywhere = pl.BlockSpec(memory_space=pl.ANY)
    scalars = pl.BlockSpec(memory_space=pltpu.SMEM)
    return pl.pallas_call(
        kernel,
        in_specs=[scalars, scalars] + [anywhere] * 24,
        out_specs=pl.BlockSpec(memory_space=pltpu.VMEM),
        scratch_shapes=[
            pltpu.VMEM((3, 4, 256, 384), jnp.bfloat16),
            pltpu.VMEM((3, 576, 384), jnp.bfloat16),
            pltpu.VMEM((8, 512, 256), jnp.float32),
            pltpu.VMEM((4, 512, 256), jnp.float32),
            pltpu.VMEM((3, 512, 256), jnp.float32),
            pltpu.SemaphoreType.DMA((3,)),
            pltpu.SemaphoreType.DMA((3,)),
        ],
        out_shape=jax.ShapeDtypeStruct((3, NTAU, 256, 128), jnp.float32),
        compiler_params=pltpu.CompilerParams(vmem_limit_bytes=24 * 2**20),
    )(shift, source, *[pltpu.with_memory_space_constraint(p, pltpu.HBM) for p in pieces])


def after(block, *others):
    return lax.optimization_barrier((block,) + others)[0]


def swap(block):
    return send(block, lambda z, yh, c, x, yl: (z, yh, 1 - c, x, yl))


def z_step(block, sign):
    return send(block, lambda z, yh, c, x, yl: (z + sign * (1 - 2 * c), yh, c, x, yl))


def x_step(block, sign):
    return send(block, lambda z, yh, c, x, yl: (z, yh, c, x + sign * (1 - 2 * c), yl))


def across_yh(block):
    return send(block, lambda z, yh, c, x, yl: (z, 1 - yh, c, x, yl))


def on_device(occ_orbitals, virt_orbitals, occ_gap, virt_gap, partner):
    z, yh, c, x, yl = (lax.axis_index(a) for a in AXES)
    shift = (-partner[:, 0]) % 64
    own = jnp.concatenate([occ_orbitals, virt_orbitals], axis=2)
    gaps = jnp.concatenate([occ_gap, virt_gap], axis=1)
    gaps = jnp.pad(gaps, ((0, 12), (0, 0)))

    def half(core):
        cut = [lax.dynamic_slice_in_dim(a, core * 128, 128, 1) for a in (occ_orbitals, virt_orbitals)]
        return jnp.concatenate([jnp.concatenate(cut, axis=2).reshape(512, 384), gaps])

    here = send(half(c), lambda z, yh, c, x, yl: (x, yl, c, x + z, yh))
    there = send(half(1 - c), lambda z, yh, c, x, yl: (x, yl, 1 - c, x + z, yh))
    cols = jnp.stack([here, there])
    cols_same, rows_same = [cols], [own]
    cols_cross = [send(cols, lambda z, yh, c, x, yl: (z, yh, c, x, 1 - yl))]
    for _ in range(3):
        rows_same.append(z_step(rows_same[-1], 1))
        cols_same.append(x_step(cols_same[-1], 1))
    rows_cross = [across_yh(after(own, cols_cross[0]))]
    cols_cross.append(x_step(after(cols_cross[0], cols_same[1]), 1))
    rows_cross.append(z_step(rows_cross[0], 1))
    cols_cross += [x_step(cols_cross[1], 1)]
    cols_cross += [x_step(cols_cross[2], 1)]
    rows_cross += [z_step(rows_cross[1], 1)]
    rows_cross += [across_yh(after(rows_same[3], rows_cross[0]))]

    def slab(at, low, core):
        return at % 4 * 4 + low * 2 + core

    pieces, slots = [], []
    for held, low in ((rows_same, yh), (rows_cross, 1 - yh)):
        for step, piece in enumerate(held):
            pieces += [piece, swap(piece)]
            slots += [slab(z + (2 * core - 1) * step, low, core) for core in (c, 1 - c)]
    for held, low in ((cols_same, yl), (cols_cross, 1 - yl)):
        for step, piece in enumerate(held):
            pieces.append(piece)
            slots += [slab(x - z + (2 * c - 1) * step, low, core) for core in (c, 1 - c)]
    slots = jnp.stack(slots)
    held = jnp.arange(16)
    source = [jnp.sum((part[:, None] == held) * held[:, None], axis=0) for part in (slots[:16], slots[16:])]
    source = jnp.concatenate(source).astype(jnp.int32)
    return polarizability(shift, source, pieces)


def solution(mesh):
    fine = Mesh(mesh.devices.reshape(4, 2, 2, 4, 2), AXES)
    kpt, row = ("z", "yh", "c"), ("x", "yl")
    in_specs = (P(kpt, row, None), P(kpt, row, None), P(kpt, None), P(kpt, None), P())
    return jax.shard_map(
        on_device, mesh=fine, in_specs=in_specs, out_specs=P(None, None, row, kpt), check_vma=False
    )
```

```python
import jax
import jax.numpy as jnp
from jax import lax
from jax.experimental import pallas as pl
from jax.experimental.pallas import tpu as pltpu
from jax.sharding import Mesh, PartitionSpec as P

AXES = ("z", "yh", "c", "x", "yl")
NTAU = 4
HEIGHT = 16
TAUS = [0.25 * 2.0**t for t in range(NTAU)]
NT_DIMS = (((1,), (1,)), ((), ()))


def routes(target):
    def linear(z, yh, c, x, yl):
        return (((z % 4) * 2 + yh) * 2 + c) * 8 + (x % 4) * 2 + yl

    return [
        (linear(z, yh, c, x, yl), linear(*target(z, yh, c, x, yl)))
        for z in range(4)
        for yh in range(2)
        for c in range(2)
        for x in range(4)
        for yl in range(2)
    ]


def send(block, target):
    return lax.ppermute(block, AXES, routes(target))


def kernel(shift, source, *refs):
    row_src, col_src, refs = refs[:16], refs[16:24], refs[24:]
    out, row_pts, col_pts, vbuf, obuf, acc, row_sems, col_sems = refs

    def row_copy(n, slot):
        return pltpu.make_async_copy(row_src[n], row_pts.at[slot], row_sems.at[slot])

    def col_copy(n, slot):
        return pltpu.make_async_copy(col_src[n // 2].at[n % 2], col_pts.at[slot, pl.ds(0, 528)], col_sems.at[slot])

    def fetch(step):
        slab, slot = lax.rem(step + 15, 16), lax.rem(step, 4)
        row_from, col_from = source[slab], source[16 + slab]
        for n in range(16):

            @pl.when(row_from == n)
            def _():
                row_copy(n, slot).start()

            @pl.when(col_from == n)
            def _():
                col_copy(n, slot).start()

    def products(step, base, obase):
        slot = lax.rem(step, 4)
        gaps = col_pts[slot, 512:528, :].astype(jnp.float32)
        factors = [jnp.exp(-gaps * TAUS[t]) for t in range(NTAU)]
        for i in range(4):
            col = col_pts[slot, i * 128 : (i + 1) * 128, :].astype(jnp.float32)
            panel = jnp.concatenate(
                [(col * factors[t][i : i + 1]).astype(jnp.bfloat16) for t in range(NTAU)], 0
            )
            vbuf[base + i] = lax.dot_general(
                panel[:, 128:], row_pts[slot, i, :, 128:], NT_DIMS, preferred_element_type=jnp.float32
            )
            if obase is not None:
                obuf[obase + i] = lax.dot_general(
                    panel[:, :128], row_pts[slot, i, :, :128], NT_DIMS, preferred_element_type=jnp.float32
                )

    def arrive(step):
        row_copy(0, lax.rem(step, 4)).wait()
        col_copy(0, lax.rem(step, 4)).wait()

    for step in range(3):
        fetch(step)
    acc[...] = jnp.zeros_like(acc)
    arrive(0)
    products(0, 4, None)

    @pl.loop(0, 8)
    def _(pair):
        @pl.when(pair < 7)
        def _():
            fetch(2 * pair + 3)
            fetch(2 * pair + 4)

        arrive(2 * pair + 1)
        arrive(2 * pair + 2)
        for part in (0, 4):
            products(2 * pair + 1 + part // 4, part, part)
            for g in range(512 // HEIGHT):
                rows = pl.ds(g * HEIGHT, HEIGHT)
                occs = [obuf[part + i, rows, :] for i in range(4)]
                for q in range(3):
                    total = acc[q, rows, :]
                    for i in range(4):
                        total = total + occs[i] * vbuf[lax.rem(part + i - shift[q] + 8, 8), rows, :]
                    acc[q, rows, :] = total

    for q in range(3):
        for t in range(NTAU):
            out[q, t] = acc[q, t * 128 : (t + 1) * 128, :].T


def polarizability(shift, source, pieces):
    anywhere = pl.BlockSpec(memory_space=pl.ANY)
    scalars = pl.BlockSpec(memory_space=pltpu.SMEM)
    return pl.pallas_call(
        kernel,
        in_specs=[scalars, scalars] + [anywhere] * 24,
        out_specs=pl.BlockSpec(memory_space=pltpu.VMEM),
        scratch_shapes=[
            pltpu.VMEM((4, 4, 256, 384), jnp.bfloat16),
            pltpu.VMEM((4, 576, 384), jnp.bfloat16),
            pltpu.VMEM((8, 512, 256), jnp.float32),
            pltpu.VMEM((8, 512, 256), jnp.float32),
            pltpu.VMEM((3, 512, 256), jnp.float32),
            pltpu.SemaphoreType.DMA((4,)),
            pltpu.SemaphoreType.DMA((4,)),
        ],
        out_shape=jax.ShapeDtypeStruct((3, NTAU, 256, 128), jnp.float32),
        compiler_params=pltpu.CompilerParams(vmem_limit_bytes=24 * 2**20),
    )(shift, source, *[pltpu.with_memory_space_constraint(p, pltpu.HBM) for p in pieces])


def after(block, *others):
    return lax.optimization_barrier((block,) + others)[0]


def swap(block):
    return send(block, lambda z, yh, c, x, yl: (z, yh, 1 - c, x, yl))


def z_step(block, sign):
    return send(block, lambda z, yh, c, x, yl: (z + sign * (1 - 2 * c), yh, c, x, yl))


def x_step(block, sign):
    return send(block, lambda z, yh, c, x, yl: (z, yh, c, x + sign * (1 - 2 * c), yl))


def across_yh(block):
    return send(block, lambda z, yh, c, x, yl: (z, 1 - yh, c, x, yl))


def on_device(occ_orbitals, virt_orbitals, occ_gap, virt_gap, partner):
    z, yh, c, x, yl = (lax.axis_index(a) for a in AXES)
    shift = (-partner[:, 0]) % 64
    gaps = jnp.concatenate([occ_gap, virt_gap], axis=1)
    gaps = jnp.pad(gaps, ((0, 12), (0, 0)))

    def half(core):
        cut = [lax.dynamic_slice_in_dim(a, core * 128, 128, 1) for a in (occ_orbitals, virt_orbitals)]
        return jnp.concatenate([jnp.concatenate(cut, axis=2).reshape(512, 384), gaps])

    halves = half(c), half(1 - c)
    own = jnp.concatenate([after(occ_orbitals, *halves), virt_orbitals], axis=2)
    here = send(halves[0], lambda z, yh, c, x, yl: (x, yl, c, x + z, yh))
    there = send(halves[1], lambda z, yh, c, x, yl: (x, yl, 1 - c, x + z, yh))
    cols = jnp.stack([here, there])
    cols_same, rows_same = [cols], [own]
    cols_cross = [send(cols, lambda z, yh, c, x, yl: (z, yh, c, x, 1 - yl))]
    for _ in range(3):
        rows_same.append(z_step(rows_same[-1], 1))
        cols_same.append(x_step(cols_same[-1], 1))
    rows_cross = [across_yh(after(own, cols_cross[0]))]
    cols_cross.append(x_step(after(cols_cross[0], cols_same[1]), 1))
    rows_cross.append(z_step(rows_cross[0], 1))
    cols_cross += [x_step(cols_cross[1], 1)]
    cols_cross += [x_step(cols_cross[2], 1)]
    rows_cross += [z_step(rows_cross[1], 1)]
    rows_cross += [across_yh(after(rows_same[3], rows_cross[0]))]

    def slab(at, low, core):
        return at % 4 * 4 + low * 2 + core

    pieces, slots = [], []
    for held, low in ((rows_same, yh), (rows_cross, 1 - yh)):
        for step, piece in enumerate(held):
            pieces += [piece, swap(piece)]
            slots += [slab(z + (2 * core - 1) * step, low, core) for core in (c, 1 - c)]
    for held, low in ((cols_same, yl), (cols_cross, 1 - yl)):
        for step, piece in enumerate(held):
            pieces.append(piece)
            slots += [slab(x - z + (2 * c - 1) * step, low, core) for core in (c, 1 - c)]
    slots = jnp.stack(slots)
    held = jnp.arange(16)
    source = [jnp.sum((part[:, None] == held) * held[:, None], axis=0) for part in (slots[:16], slots[16:])]
    source = jnp.concatenate(source).astype(jnp.int32)
    return polarizability(shift, source, pieces)


def solution(mesh):
    fine = Mesh(mesh.devices.reshape(4, 2, 2, 4, 2), AXES)
    kpt, row = ("z", "yh", "c"), ("x", "yl")
    in_specs = (P(kpt, row, None), P(kpt, row, None), P(kpt, None), P(kpt, None), P())
    return jax.shard_map(
        on_device, mesh=fine, in_specs=in_specs, out_specs=P(None, None, row, kpt), check_vma=False
    )
```

```python
import jax
import jax.numpy as jnp
from jax import lax
from jax.experimental import pallas as pl
from jax.experimental.pallas import tpu as pltpu
from jax.sharding import Mesh, PartitionSpec as P

AXES = ("z", "yh", "c", "x", "yl")
NTAU = 4
HEIGHT = 16
TAUS = [0.25 * 2.0**t for t in range(NTAU)]
NT_DIMS = (((1,), (1,)), ((), ()))


def routes(target):
    def linear(z, yh, c, x, yl):
        return (((z % 4) * 2 + yh) * 2 + c) * 8 + (x % 4) * 2 + yl

    return [
        (linear(z, yh, c, x, yl), linear(*target(z, yh, c, x, yl)))
        for z in range(4)
        for yh in range(2)
        for c in range(2)
        for x in range(4)
        for yl in range(2)
    ]


def send(block, target):
    return lax.ppermute(block, AXES, routes(target))


def kernel(shift, source, *refs):
    row_src, col_src, refs = refs[:16], refs[16:24], refs[24:]
    out, row_pts, col_pts, vbuf, obuf, acc, row_sems, col_sems = refs

    def row_copy(n, slot):
        return pltpu.make_async_copy(row_src[n], row_pts.at[slot], row_sems.at[slot])

    def col_copy(n, slot):
        return pltpu.make_async_copy(col_src[n // 2].at[n % 2], col_pts.at[slot, pl.ds(0, 528)], col_sems.at[slot])

    def fetch(step):
        slab, slot = lax.rem(step + 15, 16), lax.rem(step, 4)
        row_from, col_from = source[slab], source[16 + slab]
        for n in range(16):

            @pl.when(row_from == n)
            def _():
                row_copy(n, slot).start()

            @pl.when(col_from == n)
            def _():
                col_copy(n, slot).start()

    def products(step, base, obase):
        slot = lax.rem(step, 4)
        gaps = col_pts[slot, 512:528, :].astype(jnp.float32)
        factors = [jnp.exp(-gaps * TAUS[t]) for t in range(NTAU)]
        for i in range(4):
            col = col_pts[slot, i * 128 : (i + 1) * 128, :].astype(jnp.float32)
            panel = jnp.concatenate(
                [(col * factors[t][i : i + 1]).astype(jnp.bfloat16) for t in range(NTAU)], 0
            )
            vbuf[base + i] = lax.dot_general(
                panel[:, 128:], row_pts[slot, i, :, 128:], NT_DIMS, preferred_element_type=jnp.float32
            )
            if obase is not None:
                obuf[obase + i] = lax.dot_general(
                    panel[:, :128], row_pts[slot, i, :, :128], NT_DIMS, preferred_element_type=jnp.float32
                )

    def arrive(step):
        row_copy(0, lax.rem(step, 4)).wait()
        col_copy(0, lax.rem(step, 4)).wait()

    for step in range(3):
        fetch(step)
    acc[...] = jnp.zeros_like(acc)
    arrive(0)
    products(0, 4, None)

    @pl.loop(0, 8)
    def _(pair):
        @pl.when(pair < 7)
        def _():
            fetch(2 * pair + 3)
            fetch(2 * pair + 4)

        arrive(2 * pair + 1)
        arrive(2 * pair + 2)
        for part in (0, 4):
            products(2 * pair + 1 + part // 4, part, part)
            for g in range(512 // HEIGHT):
                rows = pl.ds(g * HEIGHT, HEIGHT)
                occs = [obuf[part + i, rows, :] for i in range(4)]
                for q in range(3):
                    total = acc[q, rows, :]
                    for i in range(4):
                        total = total + occs[i] * vbuf[lax.rem(part + i - shift[q] + 8, 8), rows, :]
                    acc[q, rows, :] = total

    for q in range(3):
        for t in range(NTAU):
            out[q, t] = acc[q, t * 128 : (t + 1) * 128, :].T


def polarizability(shift, source, pieces):
    anywhere = pl.BlockSpec(memory_space=pl.ANY)
    scalars = pl.BlockSpec(memory_space=pltpu.SMEM)
    return pl.pallas_call(
        kernel,
        in_specs=[scalars, scalars] + [anywhere] * 24,
        out_specs=pl.BlockSpec(memory_space=pltpu.VMEM),
        scratch_shapes=[
            pltpu.VMEM((4, 4, 256, 384), jnp.bfloat16),
            pltpu.VMEM((4, 576, 384), jnp.bfloat16),
            pltpu.VMEM((8, 512, 256), jnp.float32),
            pltpu.VMEM((8, 512, 256), jnp.float32),
            pltpu.VMEM((3, 512, 256), jnp.float32),
            pltpu.SemaphoreType.DMA((4,)),
            pltpu.SemaphoreType.DMA((4,)),
        ],
        out_shape=jax.ShapeDtypeStruct((3, NTAU, 256, 128), jnp.float32),
        compiler_params=pltpu.CompilerParams(vmem_limit_bytes=24 * 2**20),
    )(shift, source, *[pltpu.with_memory_space_constraint(p, pltpu.HBM) for p in pieces])


def after(block, *others):
    return lax.optimization_barrier((block,) + others)[0]


def swap(block):
    return send(block, lambda z, yh, c, x, yl: (z, yh, 1 - c, x, yl))


def z_step(block, sign):
    return send(block, lambda z, yh, c, x, yl: (z + sign * (1 - 2 * c), yh, c, x, yl))


def x_step(block, sign):
    return send(block, lambda z, yh, c, x, yl: (z, yh, c, x + sign * (1 - 2 * c), yl))


def across_yh(block):
    return send(block, lambda z, yh, c, x, yl: (z, 1 - yh, c, x, yl))


def on_device(occ_orbitals, virt_orbitals, occ_gap, virt_gap, partner):
    z, yh, c, x, yl = (lax.axis_index(a) for a in AXES)
    shift = (-partner[:, 0]) % 64
    gaps = jnp.concatenate([occ_gap, virt_gap], axis=1)
    gaps = jnp.pad(gaps, ((0, 12), (0, 0)))

    def half(core):
        cut = [lax.dynamic_slice_in_dim(a, core * 128, 128, 1) for a in (occ_orbitals, virt_orbitals)]
        return jnp.concatenate([jnp.concatenate(cut, axis=2).reshape(512, 384), gaps])

    halves = half(c), half(1 - c)
    own = jnp.concatenate([after(occ_orbitals, *halves), virt_orbitals], axis=2)
    here = send(halves[0], lambda z, yh, c, x, yl: (x, yl, c, x + z, yh))
    there = send(halves[1], lambda z, yh, c, x, yl: (x, yl, 1 - c, x + z, yh))
    cols = jnp.stack([here, there])
    cols_same, rows_same = [cols], [own]
    cols_cross = [send(cols, lambda z, yh, c, x, yl: (z, yh, c, x, 1 - yl))]
    for _ in range(3):
        rows_same.append(z_step(rows_same[-1], 1))
        cols_same.append(x_step(cols_same[-1], 1))
    rows_cross = [across_yh(after(own, cols_cross[0]))]
    cols_cross.append(x_step(cols_cross[0], 1))
    rows_cross.append(z_step(rows_cross[0], 1))
    cols_cross += [x_step(cols_cross[1], 1)]
    cols_cross += [x_step(cols_cross[2], 1)]
    rows_cross += [z_step(rows_cross[1], 1)]
    rows_cross += [across_yh(rows_same[3])]

    def slab(at, low, core):
        return at % 4 * 4 + low * 2 + core

    pieces, slots = [], []
    for held, low in ((rows_same, yh), (rows_cross, 1 - yh)):
        for step, piece in enumerate(held):
            pieces += [piece, swap(piece)]
            slots += [slab(z + (2 * core - 1) * step, low, core) for core in (c, 1 - c)]
    for held, low in ((cols_same, yl), (cols_cross, 1 - yl)):
        for step, piece in enumerate(held):
            pieces.append(piece)
            slots += [slab(x - z + (2 * c - 1) * step, low, core) for core in (c, 1 - c)]
    slots = jnp.stack(slots)
    held = jnp.arange(16)
    source = [jnp.sum((part[:, None] == held) * held[:, None], axis=0) for part in (slots[:16], slots[16:])]
    source = jnp.concatenate(source).astype(jnp.int32)
    return polarizability(shift, source, pieces)


def solution(mesh):
    fine = Mesh(mesh.devices.reshape(4, 2, 2, 4, 2), AXES)
    kpt, row = ("z", "yh", "c"), ("x", "yl")
    in_specs = (P(kpt, row, None), P(kpt, row, None), P(kpt, None), P(kpt, None), P())
    return jax.shard_map(
        on_device, mesh=fine, in_specs=in_specs, out_specs=P(None, None, row, kpt), check_vma=False
    )
```

```python
import jax
import jax.numpy as jnp
from jax import lax
from jax.experimental import pallas as pl
from jax.experimental.pallas import tpu as pltpu
from jax.sharding import Mesh, PartitionSpec as P

AXES = ("z", "yh", "c", "x", "yl")
NTAU = 4
HEIGHT = 16
TAUS = [0.25 * 2.0**t for t in range(NTAU)]
NT_DIMS = (((1,), (1,)), ((), ()))


def routes(target):
    def linear(z, yh, c, x, yl):
        return (((z % 4) * 2 + yh) * 2 + c) * 8 + (x % 4) * 2 + yl

    return [
        (linear(z, yh, c, x, yl), linear(*target(z, yh, c, x, yl)))
        for z in range(4)
        for yh in range(2)
        for c in range(2)
        for x in range(4)
        for yl in range(2)
    ]


def send(block, target):
    return lax.ppermute(block, AXES, routes(target))


def kernel(shift, source, *refs):
    row_src, col_src, refs = refs[:16], refs[16:24], refs[24:]
    out, row_pts, col_pts, vbuf, obuf, acc, row_sems, col_sems = refs

    def row_copy(n, slot):
        return pltpu.make_async_copy(row_src[n], row_pts.at[slot], row_sems.at[slot])

    def col_copy(n, slot):
        return pltpu.make_async_copy(col_src[n // 2].at[n % 2], col_pts.at[slot, pl.ds(0, 528)], col_sems.at[slot])

    def fetch(step):
        slab, slot = lax.rem(step + 15, 16), lax.rem(step, 4)
        row_from, col_from = source[slab], source[16 + slab]
        for start in range(0, 16, 4):

            @pl.when((row_from >= start) & (row_from < start + 4))
            def _():
                for n in range(start, start + 4):

                    @pl.when(row_from == n)
                    def _():
                        row_copy(n, slot).start()

            @pl.when((col_from >= start) & (col_from < start + 4))
            def _():
                for n in range(start, start + 4):

                    @pl.when(col_from == n)
                    def _():
                        col_copy(n, slot).start()

    def products(step, base, obase):
        slot = lax.rem(step, 4)
        gaps = col_pts[slot, 512:528, :].astype(jnp.float32)
        factors = [jnp.exp(-gaps * TAUS[t]) for t in range(NTAU)]
        for i in range(4):
            col = col_pts[slot, i * 128 : (i + 1) * 128, :].astype(jnp.float32)
            panel = jnp.concatenate(
                [(col * factors[t][i : i + 1]).astype(jnp.bfloat16) for t in range(NTAU)], 0
            )
            vbuf[base + i] = lax.dot_general(
                panel[:, 128:], row_pts[slot, i, :, 128:], NT_DIMS, preferred_element_type=jnp.float32
            )
            if obase is not None:
                obuf[obase + i] = lax.dot_general(
                    panel[:, :128], row_pts[slot, i, :, :128], NT_DIMS, preferred_element_type=jnp.float32
                )

    def arrive(step):
        row_copy(0, lax.rem(step, 4)).wait()
        col_copy(0, lax.rem(step, 4)).wait()

    for step in range(3):
        fetch(step)
    acc[...] = jnp.zeros_like(acc)
    arrive(0)
    products(0, 4, None)

    @pl.loop(0, 8)
    def _(pair):
        @pl.when(pair < 7)
        def _():
            fetch(2 * pair + 3)
            fetch(2 * pair + 4)

        arrive(2 * pair + 1)
        arrive(2 * pair + 2)
        for part in (0, 4):
            products(2 * pair + 1 + part // 4, part, part)
            for g in range(512 // HEIGHT):
                rows = pl.ds(g * HEIGHT, HEIGHT)
                occs = [obuf[part + i, rows, :] for i in range(4)]
                for q in range(3):
                    total = acc[q, rows, :]
                    for i in range(4):
                        total = total + occs[i] * vbuf[lax.rem(part + i - shift[q] + 8, 8), rows, :]
                    acc[q, rows, :] = total

    for q in range(3):
        for t in range(NTAU):
            out[q, t] = acc[q, t * 128 : (t + 1) * 128, :].T


def polarizability(shift, source, pieces):
    anywhere = pl.BlockSpec(memory_space=pl.ANY)
    scalars = pl.BlockSpec(memory_space=pltpu.SMEM)
    return pl.pallas_call(
        kernel,
        in_specs=[scalars, scalars] + [anywhere] * 24,
        out_specs=pl.BlockSpec(memory_space=pltpu.VMEM),
        scratch_shapes=[
            pltpu.VMEM((4, 4, 256, 384), jnp.bfloat16),
            pltpu.VMEM((4, 576, 384), jnp.bfloat16),
            pltpu.VMEM((8, 512, 256), jnp.float32),
            pltpu.VMEM((8, 512, 256), jnp.float32),
            pltpu.VMEM((3, 512, 256), jnp.float32),
            pltpu.SemaphoreType.DMA((4,)),
            pltpu.SemaphoreType.DMA((4,)),
        ],
        out_shape=jax.ShapeDtypeStruct((3, NTAU, 256, 128), jnp.float32),
        compiler_params=pltpu.CompilerParams(vmem_limit_bytes=24 * 2**20),
    )(shift, source, *[pltpu.with_memory_space_constraint(p, pltpu.HBM) for p in pieces])


def after(block, *others):
    return lax.optimization_barrier((block,) + others)[0]


def swap(block):
    return send(block, lambda z, yh, c, x, yl: (z, yh, 1 - c, x, yl))


def z_step(block, sign):
    return send(block, lambda z, yh, c, x, yl: (z + sign * (1 - 2 * c), yh, c, x, yl))


def x_step(block, sign):
    return send(block, lambda z, yh, c, x, yl: (z, yh, c, x + sign * (1 - 2 * c), yl))


def across_yh(block):
    return send(block, lambda z, yh, c, x, yl: (z, 1 - yh, c, x, yl))


def on_device(occ_orbitals, virt_orbitals, occ_gap, virt_gap, partner):
    z, yh, c, x, yl = (lax.axis_index(a) for a in AXES)
    shift = (-partner[:, 0]) % 64
    gaps = jnp.concatenate([occ_gap, virt_gap], axis=1)
    gaps = jnp.pad(gaps, ((0, 12), (0, 0)))

    def half(core):
        cut = [lax.dynamic_slice_in_dim(a, core * 128, 128, 1) for a in (occ_orbitals, virt_orbitals)]
        return jnp.concatenate([jnp.concatenate(cut, axis=2).reshape(512, 384), gaps])

    halves = half(c), half(1 - c)
    own = jnp.concatenate([after(occ_orbitals, *halves), virt_orbitals], axis=2)
    here = send(halves[0], lambda z, yh, c, x, yl: (x, yl, c, x + z, yh))
    there = send(halves[1], lambda z, yh, c, x, yl: (x, yl, 1 - c, x + z, yh))
    cols = jnp.stack([here, there])
    cols_same, rows_same = [cols], [own]
    cols_cross = [send(cols, lambda z, yh, c, x, yl: (z, yh, c, x, 1 - yl))]
    for _ in range(3):
        rows_same.append(z_step(rows_same[-1], 1))
        cols_same.append(x_step(cols_same[-1], 1))
    rows_cross = [across_yh(after(own, cols_cross[0]))]
    cols_cross.append(x_step(cols_cross[0], 1))
    rows_cross.append(z_step(rows_cross[0], 1))
    cols_cross += [x_step(cols_cross[1], 1)]
    cols_cross += [x_step(cols_cross[2], 1)]
    rows_cross += [z_step(rows_cross[1], 1)]
    rows_cross += [across_yh(rows_same[3])]

    def slab(at, low, core):
        return at % 4 * 4 + low * 2 + core

    pieces, slots = [], []
    for held, low in ((rows_same, yh), (rows_cross, 1 - yh)):
        for step, piece in enumerate(held):
            pieces += [piece, swap(piece)]
            slots += [slab(z + (2 * core - 1) * step, low, core) for core in (c, 1 - c)]
    for held, low in ((cols_same, yl), (cols_cross, 1 - yl)):
        for step, piece in enumerate(held):
            pieces.append(piece)
            slots += [slab(x - z + (2 * c - 1) * step, low, core) for core in (c, 1 - c)]
    slots = jnp.stack(slots)
    held = jnp.arange(16)
    source = [jnp.sum((part[:, None] == held) * held[:, None], axis=0) for part in (slots[:16], slots[16:])]
    source = jnp.concatenate(source).astype(jnp.int32)
    return polarizability(shift, source, pieces)


def solution(mesh):
    fine = Mesh(mesh.devices.reshape(4, 2, 2, 4, 2), AXES)
    kpt, row = ("z", "yh", "c"), ("x", "yl")
    in_specs = (P(kpt, row, None), P(kpt, row, None), P(kpt, None), P(kpt, None), P())
    return jax.shard_map(
        on_device, mesh=fine, in_specs=in_specs, out_specs=P(None, None, row, kpt), check_vma=False
    )
```
